512 devices in a mesh: row: 64 (over z, x), col: 8 (over y, core).
Axes of the slice: x: 4, y: 4, z: 16, core: 2. Of those that a mesh axis runs over, the one named last changes fastest.
Arguments:
- half_tensor: float32 [64, 400, 4096], P('row', 'col'), may hold values from -0.0390625 to 0.0390625
- earlier_blocks: float32 [64, 512, 512], P('row'), may hold values from -6 to 6
Outputs:
- exchange_blocks: float32 [64, 512, 512], P('row')
The draws below stay inside these ranges and needn't reach their ends.
All inputs are finite; a program needn't handle non-finite values.
Results may differ from the reference program's by a relative error of at most 0.000068.
Values sent between devices are 32-bit elements; how exact they have to be, the bound alone decides.
A program may use at most 128 MiB of HBM per device.

```python
import jax
import jax.numpy as jnp
from jax import lax

BASIS = 4096
OCC = 400
AUX = 64
GRID = 8
WIDTH = 512


def shard_levels(key, extent, pieces, low, high):
    def one(position, blocks):
        steps = jax.random.uniform(jax.random.fold_in(jax.random.fold_in(key, 6), position), (blocks,), jnp.float32, low / len(pieces), high / len(pieces))
        return jnp.repeat(jnp.exp(steps), extent[position] // blocks).reshape((-1,) + (1,) * (len(extent) - position - 1))

    factor_of = one(*pieces[0])
    for cut in pieces[1:]:
        factor_of = factor_of * one(*cut)
    return factor_of


def centred(key, dims, width, limit, pieces=(), dtype=jnp.bfloat16):
    level = shard_levels(key, dims, pieces, -0.22, 0.18) if pieces else 1.0
    result = jax.random.normal(key, dims, jnp.float32) * width * level
    return jnp.minimum(jnp.maximum(result, -limit), limit).astype(dtype)


def setup_inputs(seed: int = 0) -> dict:
    streams_of = jax.random.split(jax.random.key(seed), 3)
    return {
        "half_tensor": centred(streams_of[0], (AUX, OCC, BASIS), (AUX * OCC) ** -0.5, 0.0390625, ((0, 64), (1, 8)), jnp.float32),
        "earlier_blocks": centred(streams_of[1], (GRID * GRID, WIDTH, WIDTH), 0.5, 6.0, ((0, 64),), jnp.float32),
    }


def reference(half_tensor, earlier_blocks):
    flat = half_tensor.reshape(AUX * OCC, BASIS)
    slab_product = jnp.dot(flat.T, flat, preferred_element_type=jnp.float32, precision=lax.Precision.HIGHEST)
    blocks = slab_product.reshape(GRID, WIDTH, GRID, WIDTH).transpose(0, 2, 1, 3).reshape(GRID * GRID, WIDTH, WIDTH)
    return earlier_blocks + blocks
```

```python
import jax
import jax.numpy as jnp
from jax import lax
from jax.experimental import pallas as pl
from jax.experimental.pallas import tpu as pltpu
from jax.sharding import PartitionSpec as P

MESH = pl.DeviceIdType.MESH
F32 = jnp.float32
BF16 = jnp.bfloat16

NX, NY, NZ, NK = 4, 4, 16, 2
ROWS = 50
PIECE = ROWS * 8
DEPTH = 16 * ROWS
PADDED = 896
HALF = 25 * 8
QUARTER = 128
OWN = 64
WIDTH = 512


def kernel(
    half_ref,
    earlier_ref,
    out_ref,
    col_send,
    row_send,
    col_buf,
    row_buf,
    row_hi,
    row_lo,
    col_hi,
    col_lo,
    tile,
    sibling_tile,
    up_send,
    down_send,
    up_recv,
    down_recv,
    c_ssem,
    c_rsem,
    r_ssem,
    r_rsem,
    s_ssem,
    s_rsem,
    up_ssem,
    up_rsem,
    down_ssem,
    down_rsem,
    o_ssem,
    o_rsem,
):
    r = lax.axis_index("row")
    c = lax.axis_index("col")
    z, x, y, k = r // NX, r % NX, c // NK, c % NK

    def device(dz=0, dx=0, dy=0, dk=0):
        return (
            lax.rem(z + dz, NZ) * NX + lax.rem(x + dx, NX),
            lax.rem(y + dy, NY) * NK + lax.rem(k + dk, NK),
        )

    def remote(src, dst, ssem, rsem, to):
        return pltpu.make_async_remote_copy(
            src_ref=src, dst_ref=dst, send_sem=ssem, recv_sem=rsem, device_id=to, device_id_type=MESH
        )

    peers = [device(dx=j) for j in range(1, NX)] + [device(dy=j) for j in range(1, NY)]
    peers += [device(dz=1), device(dz=NZ - 1), device(dk=1)]
    barrier = pltpu.get_barrier_semaphore()
    for peer in peers:
        pl.semaphore_signal(barrier, inc=1, device_id=peer, device_id_type=MESH)

    for i in range(7):
        n = min(8, ROWS - 8 * i)
        for t in range(32):
            g, q = t // 4, t % 4
            v = half_ref[0, 8 * i : 8 * i + n, 128 * t : 128 * t + 128]
            col_send[g % 4, pl.ds(64 * i + (g // 4) * 4 + q, n, stride=8), :] = v
            row_send[q, pl.ds(64 * i + g, n, stride=8), :] = v
    col_buf[pl.ds(0, PIECE), :] = col_send[x]
    row_buf[pl.ds(0, PIECE), :] = row_send[y]
    pad = jnp.zeros((8 * (PADDED - DEPTH), 128), F32)
    col_buf[pl.ds(8 * DEPTH, 8 * (PADDED - DEPTH)), :] = pad
    row_buf[pl.ds(8 * DEPTH, 8 * (PADDED - DEPTH)), :] = pad

    pl.semaphore_wait(barrier, len(peers))

    def slot(buf, dx, dy, part=None):
        base = (dx * 4 + dy) * PIECE
        if part is None:
            return buf.at[pl.ds(base, PIECE), :]
        return buf.at[pl.ds(base + part * HALF, HALF), :]

    sends = []

    def go(copy):
        copy.start()
        sends.append(copy)

    for j in (1, 3, 2):
        go(remote(col_send.at[lax.rem(x + j, NX)], slot(col_buf, 4 - j, 0), c_ssem.at[j, 0], c_rsem.at[4 - j, 0], device(dx=j)))
        go(remote(row_send.at[lax.rem(y + j, NY)], slot(row_buf, 0, 4 - j), r_ssem.at[j, 0], r_rsem.at[0, 4 - j], device(dy=j)))

    def spread(a):
        go(remote(slot(col_buf, a, 0), slot(col_buf, a, 3), c_ssem.at[a, 1], c_rsem.at[a, 3], device(dy=1)))
        go(remote(slot(row_buf, 0, a), slot(row_buf, 3, a), r_ssem.at[a, 1], r_rsem.at[3, a], device(dx=1)))
        go(remote(slot(col_buf, a, 0), slot(col_buf, a, 1), c_ssem.at[a, 2], c_rsem.at[a, 1], device(dy=3)))
        go(remote(slot(row_buf, 0, a), slot(row_buf, 1, a), r_ssem.at[a, 2], r_rsem.at[1, a], device(dx=3)))

    def arrived(dst, rsem):
        remote(dst, dst, rsem, rsem, device(dy=1)).wait_recv()

    def forward(a):
        arrived(slot(col_buf, a, 3), c_rsem.at[a, 3])
        go(remote(slot(col_buf, a, 3, 0), slot(col_buf, a, 2, 0), c_ssem.at[a, 3], c_rsem.at[a, 2], device(dy=1)))
        arrived(slot(row_buf, 3, a), r_rsem.at[3, a])
        go(remote(slot(row_buf, 3, a, 0), slot(row_buf, 2, a, 0), r_ssem.at[a, 3], r_rsem.at[2, a], device(dx=1)))
        arrived(slot(col_buf, a, 1), c_rsem.at[a, 1])
        go(remote(slot(col_buf, a, 1, 1), slot(col_buf, a, 2, 1), c_ssem.at[a, 4], c_rsem.at[a, 4], device(dy=3)))
        arrived(slot(row_buf, 1, a), r_rsem.at[1, a])
        go(remote(slot(row_buf, 1, a, 1), slot(row_buf, 2, a, 1), r_ssem.at[a, 4], r_rsem.at[4, a], device(dx=3)))

    spread(0)
    for a in (3, 1, 2):
        arrived(slot(col_buf, a, 0), c_rsem.at[a, 0])
        arrived(slot(row_buf, 0, a), r_rsem.at[0, a])
        spread(a)
        if a == 3:
            forward(0)
    for a in (3, 1, 2):
        forward(a)
    for a in range(4):
        arrived(slot(col_buf, a, 2, 0), c_rsem.at[a, 2])
        arrived(slot(row_buf, 2, a, 0), r_rsem.at[2, a])
        arrived(slot(col_buf, a, 2, 1), c_rsem.at[a, 4])
        arrived(slot(row_buf, 2, a, 1), r_rsem.at[4, a])

    for s in range(8):
        v = col_buf[pl.ds(s, PADDED, stride=8), :]
        hi = v.astype(BF16)
        col_hi[:, 128 * s : 128 * s + 128] = hi
        col_lo[:, 128 * s : 128 * s + 128] = (v - hi.astype(F32)).astype(BF16)
        v = row_buf[pl.ds(s, PADDED, stride=8), :].T
        hi = v.astype(BF16)
        row_hi[128 * s : 128 * s + 128, :] = hi
        row_lo[128 * s : 128 * s + 128, :] = (v - hi.astype(F32)).astype(BF16)

    @pl.loop(0, 4)
    def _(j):
        cols = pl.ds(pl.multiple_of(j * 256, 256), 256)
        acc = jnp.dot(row_lo[...], col_hi[:, cols], preferred_element_type=F32)
        acc += jnp.dot(row_hi[...], col_lo[:, cols], preferred_element_type=F32)
        acc += jnp.dot(row_hi[...], col_hi[:, cols], preferred_element_type=F32)
        for u in range(8):
            tile[2 * u + j // 2, :, pl.ds(pl.multiple_of((j % 2) * 256, 256), 256)] = acc[128 * u : 128 * u + 128]

    mine = pl.ds(pl.multiple_of(k * OWN, OWN), OWN)
    other = pl.ds(pl.multiple_of((1 - k) * OWN, OWN), OWN)

    def dest(dz):
        return lax.rem(z + dz, NZ)

    order = [8]
    for s in range(1, 8):
        order += [8 + s, 8 - s]
    order += [0]
    for i, dz in enumerate(order):
        go(remote(tile.at[dest(dz), other, :], sibling_tile.at[i], s_ssem.at[i], s_rsem.at[i], device(dk=1)))

    def own_sum(dz):
        i = order.index(dz)
        arrived(sibling_tile.at[i], s_rsem.at[i])
        return tile[dest(dz), mine, :] + sibling_tile[i]

    for s in range(8):
        total = own_sum(8 - s)
        if s > 0:
            arrived(up_recv.at[s - 1], up_rsem.at[s - 1])
            total += up_recv[s - 1]
        up_send[s] = total
        go(remote(up_send.at[s], up_recv.at[s], up_ssem.at[s], up_rsem.at[s], device(dz=1)))
        if s < 7:
            total = own_sum(9 + s)
            if s > 0:
                arrived(down_recv.at[s - 1], down_rsem.at[s - 1])
                total += down_recv[s - 1]
            down_send[s] = total
            go(remote(down_send.at[s], down_recv.at[s], down_ssem.at[s], down_rsem.at[s], device(dz=NZ - 1)))

    def rows_of(dy, dk):
        start = lax.rem(y + dy, NY) * QUARTER + lax.rem(k + dk, NK) * OWN
        return pl.ds(pl.multiple_of(start, OWN), OWN)

    here = rows_of(0, 0)
    total = own_sum(0) + earlier_ref[0, here, :]
    arrived(down_recv.at[6], down_rsem.at[6])
    total += down_recv[6]
    arrived(up_recv.at[7], up_rsem.at[7])
    total += up_recv[7]
    out_ref[0, here, :] = total

    for j in (1, 3, 2):
        go(remote(out_ref.at[0, here, :], out_ref.at[0, here, :], o_ssem.at[j], o_rsem.at[4 - j], device(dy=j)))
    for j in (0, 3, 1, 2):
        rows = rows_of(j, 0)
        if j:
            arrived(out_ref.at[0, rows, :], o_rsem.at[j])
        go(remote(out_ref.at[0, rows, :], out_ref.at[0, rows, :], o_ssem.at[4 + j], o_rsem.at[4 + j], device(dk=1)))
    for j in range(4):
        arrived(out_ref.at[0, rows_of(j, 1), :], o_rsem.at[4 + j])
    for copy in sends:
        copy.wait_send()


def body(half_tensor, earlier_blocks):
    vmem = pl.BlockSpec(memory_space=pltpu.VMEM)
    dma = pltpu.SemaphoreType.DMA
    return pl.pallas_call(
        kernel,
        out_shape=jax.ShapeDtypeStruct(earlier_blocks.shape, F32),
        in_specs=[vmem, vmem],
        out_specs=vmem,
        scratch_shapes=[
            pltpu.VMEM((4, PIECE, 128), F32),
            pltpu.VMEM((4, PIECE, 128), F32),
            pltpu.VMEM((8 * PADDED, 128), F32),
            pltpu.VMEM((8 * PADDED, 128), F32),
            pltpu.VMEM((1024, PADDED), BF16),
            pltpu.VMEM((1024, PADDED), BF16),
            pltpu.VMEM((PADDED, 1024), BF16),
            pltpu.VMEM((PADDED, 1024), BF16),
            pltpu.VMEM((NZ, QUARTER, WIDTH), F32),
            pltpu.VMEM((NZ, OWN, WIDTH), F32),
            pltpu.VMEM((8, OWN, WIDTH), F32),
            pltpu.VMEM((7, OWN, WIDTH), F32),
            pltpu.VMEM((8, OWN, WIDTH), F32),
            pltpu.VMEM((7, OWN, WIDTH), F32),
            dma((4, 5)),
            dma((5, 5)),
            dma((4, 5)),
            dma((5, 5)),
            dma((NZ,)),
            dma((NZ,)),
            dma((8,)),
            dma((8,)),
            dma((7,)),
            dma((7,)),
            dma((8,)),
            dma((8,)),
        ],
        compiler_params=pltpu.CompilerParams(
            collective_id=0, has_side_effects=True, vmem_limit_bytes=48 * 2**20
        ),
        cost_estimate=pl.CostEstimate(
            flops=6 * 1024 * 1024 * DEPTH, bytes_accessed=3 * 2**20, transcendentals=0
        ),
    )(half_tensor, earlier_blocks)


def solution(mesh):
    return jax.shard_map(
        body,
        mesh=mesh,
        in_specs=(P("row", "col", None), P("row", None, None)),
        out_specs=P("row", None, None),
        check_vma=False,
    )
```

```python
import jax
import jax.numpy as jnp
from jax import lax
from jax.experimental import pallas as pl
from jax.experimental.pallas import tpu as pltpu
from jax.sharding import PartitionSpec as P

MESH = pl.DeviceIdType.MESH
F32 = jnp.float32
BF16 = jnp.bfloat16

NX, NY, NZ, NK = 4, 4, 16, 2
ROWS = 50
PIECE = ROWS * 8
HALF = 25 * 8
DEPTH = 256
QUARTER = 128
OWN = 64
CHUNKS = 2
PART = OWN // CHUNKS
WIDTH = 512

GROUPS = (
    ((0, 0), (0, 3), (3, 0), (3, 3)),
    ((0, 1), (1, 0), (1, 1), (1, 3), (3, 1)),
    ((0, 2), (2, 0), (3, 2), (2, 3)),
    ((1, 2), (2, 1), (2, 2)),
)
PLACE = {source: (g, i) for g, group in enumerate(GROUPS) for i, source in enumerate(group)}
OFFSETS = (4, 3, 5, 2, 6, 1, 7, 0)


def kernel(
    half_hbm,
    earlier_hbm,
    out_ref,
    half,
    earlier,
    col_send,
    row_send,
    col_buf,
    row_buf,
    row_hi,
    row_lo,
    col_hi,
    col_lo,
    tile,
    sibling_tile,
    up_send,
    down_send,
    up_recv,
    down_recv,
    in_sem,
    c_ssem,
    c_rsem,
    r_ssem,
    r_rsem,
    s_ssem,
    s_rsem,
    up_ssem,
    up_rsem,
    down_ssem,
    down_rsem,
    o_ssem,
    o_rsem,
):
    r = lax.axis_index("row")
    c = lax.axis_index("col")
    z, x, y, k = r // NX, r % NX, c // NK, c % NK
    odd = z % 2

    def device(dz=0, dx=0, dy=0, dk=0):
        return (
            lax.rem(z + dz, NZ) * NX + lax.rem(x + dx, NX),
            lax.rem(y + dy, NY) * NK + lax.rem(k + dk, NK),
        )

    def remote(src, dst, ssem, rsem, to):
        return pltpu.make_async_remote_copy(
            src_ref=src, dst_ref=dst, send_sem=ssem, recv_sem=rsem, device_id=to, device_id_type=MESH
        )

    def rows_of(dy, dk, chunk=None):
        start = lax.rem(y + dy, NY) * QUARTER + lax.rem(k + dk, NK) * OWN
        if chunk is None:
            return pl.ds(pl.multiple_of(start, OWN), OWN)
        return pl.ds(pl.multiple_of(start + chunk * PART, PART), PART)

    load = pltpu.make_async_copy(half_hbm, half, in_sem.at[0])
    load.start()
    load_earlier = pltpu.make_async_copy(earlier_hbm.at[0, rows_of(0, 0), :], earlier, in_sem.at[1])
    load_earlier.start()

    peers = [device(dx=j) for j in range(1, NX)] + [device(dy=j) for j in range(1, NY)]
    peers += [device(dz=1), device(dz=NZ - 1), device(dk=1)]
    barrier = pltpu.get_barrier_semaphore()
    for peer in peers:
        pl.semaphore_signal(barrier, inc=1, device_id=peer, device_id_type=MESH)

    def slot(buf, dx, dy, part=None):
        group, i = PLACE[dx, dy]
        if part is None:
            return buf.at[group, pl.ds(i * PIECE, PIECE), :]
        return buf.at[group, pl.ds(i * PIECE + part * HALF, HALF), :]

    for g, group in enumerate(GROUPS):
        filled = len(group) * PIECE
        pad = jnp.zeros((8 * DEPTH - filled, 128), F32)
        col_buf[g, pl.ds(filled, 8 * DEPTH - filled), :] = pad
        row_buf[g, pl.ds(filled, 8 * DEPTH - filled), :] = pad

    load.wait()
    for i in range(ROWS):
        for n in range(4):
            low = half[pl.ds(32 * i + 4 * n, 4), :]
            high = half[pl.ds(32 * i + 16 + 4 * n, 4), :]
            col_send[n, pl.ds(8 * i, 4), :] = low
            col_send[n, pl.ds(8 * i + 4, 4), :] = high
            row_send[n, pl.ds(8 * i, 8), :] = half[pl.ds(32 * i + n, 8, stride=4), :]

    pl.semaphore_wait(barrier, len(peers))

    sends = []

    def go(copy):
        copy.start()
        sends.append(copy)

    for j in (1, 3, 2):
        go(remote(col_send.at[lax.rem(x + j, NX)], slot(col_buf, 4 - j, 0), c_ssem.at[j, 0], c_rsem.at[4 - j, 0], device(dx=j)))
        go(remote(row_send.at[lax.rem(y + j, NY)], slot(row_buf, 0, 4 - j), r_ssem.at[j, 0], r_rsem.at[0, 4 - j], device(dy=j)))
    slot(col_buf, 0, 0)[...] = col_send[x]
    slot(row_buf, 0, 0)[...] = row_send[y]

    def spread(a):
        go(remote(slot(col_buf, a, 0), slot(col_buf, a, 3), c_ssem.at[a, 1], c_rsem.at[a, 3], device(dy=1)))
        go(remote(slot(row_buf, 0, a), slot(row_buf, 3, a), r_ssem.at[a, 1], r_rsem.at[3, a], device(dx=1)))
        go(remote(slot(col_buf, a, 0), slot(col_buf, a, 1), c_ssem.at[a, 2], c_rsem.at[a, 1], device(dy=3)))
        go(remote(slot(row_buf, 0, a), slot(row_buf, 1, a), r_ssem.at[a, 2], r_rsem.at[1, a], device(dx=3)))

    def arrived(dst, rsem):
        remote(dst, dst, rsem, rsem, device(dy=1)).wait_recv()

    def forward(a):
        arrived(slot(col_buf, a, 3), c_rsem.at[a, 3])
        go(remote(slot(col_buf, a, 3, 0), slot(col_buf, a, 2, 0), c_ssem.at[a, 3], c_rsem.at[a, 2], device(dy=1)))
        arrived(slot(row_buf, 3, a), r_rsem.at[3, a])
        go(remote(slot(row_buf, 3, a, 0), slot(row_buf, 2, a, 0), r_ssem.at[a, 3], r_rsem.at[2, a], device(dx=1)))
        arrived(slot(col_buf, a, 1), c_rsem.at[a, 1])
        go(remote(slot(col_buf, a, 1, 1), slot(col_buf, a, 2, 1), c_ssem.at[a, 4], c_rsem.at[a, 4], device(dy=3)))
        arrived(slot(row_buf, 1, a), r_rsem.at[1, a])
        go(remote(slot(row_buf, 1, a, 1), slot(row_buf, 2, a, 1), r_ssem.at[a, 4], r_rsem.at[4, a], device(dx=3)))

    def finish(a):
        arrived(slot(col_buf, a, 2, 0), c_rsem.at[a, 2])
        arrived(slot(row_buf, 2, a, 0), r_rsem.at[2, a])
        arrived(slot(col_buf, a, 2, 1), c_rsem.at[a, 4])
        arrived(slot(row_buf, 2, a, 1), r_rsem.at[4, a])

    def split(g):
        for n in range(8):
            v = col_buf[g, pl.ds(n, DEPTH, stride=8), :]
            hi = v.astype(BF16)
            col_hi[:, 128 * n : 128 * n + 128] = hi
            col_lo[:, 128 * n : 128 * n + 128] = (v - hi.astype(F32)).astype(BF16)
            offset = odd * ((8 - OFFSETS[n]) % 8) + (1 - odd) * OFFSETS[n]
            u = lax.rem(z // 2 + offset, 8)
            v = row_buf[g, pl.ds(u, DEPTH, stride=8), :].T
            hi = v.astype(BF16)
            row_hi[128 * n : 128 * n + 128, :] = hi
            row_lo[128 * n : 128 * n + 128, :] = (v - hi.astype(F32)).astype(BF16)

    def product(rows, cols):
        acc = jnp.dot(row_lo[rows, :], col_hi[:, cols], preferred_element_type=F32)
        acc += jnp.dot(row_hi[rows, :], col_lo[:, cols], preferred_element_type=F32)
        acc += jnp.dot(row_hi[rows, :], col_hi[:, cols], preferred_element_type=F32)
        return acc

    def multiply(g):
        split(g)

        @pl.loop(0, 4)
        def _(j):
            acc = product(slice(None), pl.ds(pl.multiple_of(j * 256, 256), 256))
            cols = pl.ds(pl.multiple_of((j % 2) * 256, 256), 256)
            for n in range(8):
                part = acc[128 * n : 128 * n + 128]
                if g > 0:
                    part += tile[2 * n + j // 2, :, cols]
                tile[2 * n + j // 2, :, cols] = part

    spread(0)
    for a in (3, 1, 2):
        arrived(slot(col_buf, a, 0), c_rsem.at[a, 0])
        arrived(slot(row_buf, 0, a), r_rsem.at[0, a])
        spread(a)
        if a == 3:
            forward(0)
    forward(3)
    multiply(0)
    forward(1)
    multiply(1)
    forward(2)
    finish(0)
    finish(3)
    multiply(2)
    finish(1)
    finish(2)
    split(3)

    other = pl.ds(pl.multiple_of((1 - k) * OWN, OWN), OWN)

    def last(m):
        for j in range(4):
            acc = product(slice(256 * m, 256 * m + 256), slice(256 * j, 256 * j + 256))
            cols = slice((j % 2) * 256, (j % 2) * 256 + 256)
            for n in range(2):
                tile[4 * m + 2 * n + j // 2, :, cols] += acc[128 * n : 128 * n + 128]
        for n in (2 * m, 2 * m + 1):
            go(remote(tile.at[pl.ds(2 * n, 2), other, :], sibling_tile.at[pl.ds(2 * n, 2)], s_ssem.at[n], s_rsem.at[n], device(dk=1)))

    def sibling_arrived(n):
        arrived(sibling_tile.at[pl.ds(2 * n, 2)], s_rsem.at[n])

    def own_sum(dz, chunk):
        def index(distance, flip):
            n = OFFSETS.index(distance // 2)
            return 2 * n + (distance % 2 if not flip else 1 - distance % 2)

        i = odd * index((NZ - dz) % NZ, True) + (1 - odd) * index(dz, False)
        mine = pl.ds(pl.multiple_of(k * OWN + chunk * PART, PART), PART)
        return tile[i, mine, :] + sibling_tile[i, pl.ds(chunk * PART, PART), :]

    def step(s):
        for ch in range(CHUNKS):
            total = own_sum(8 - s, ch)
            if s > 0:
                arrived(up_recv.at[s - 1, ch], up_rsem.at[s - 1, ch])
                total += up_recv[s - 1, ch]
            up_send[s, ch] = total
            go(remote(up_send.at[s, ch], up_recv.at[s, ch], up_ssem.at[s, ch], up_rsem.at[s, ch], device(dz=1)))
            if s < 7:
                total = own_sum(9 + s, ch)
                if s > 0:
                    arrived(down_recv.at[s - 1, ch], down_rsem.at[s - 1, ch])
                    total += down_recv[s - 1, ch]
                down_send[s, ch] = total
                go(remote(down_send.at[s, ch], down_recv.at[s, ch], down_ssem.at[s, ch], down_rsem.at[s, ch], device(dz=NZ - 1)))

    last(0)
    last(1)
    sibling_arrived(0)
    sibling_arrived(1)
    step(0)
    last(2)
    sibling_arrived(2)
    step(1)
    last(3)
    sibling_arrived(3)
    step(2)
    for s in range(3, 8):
        if s < 7:
            sibling_arrived(s + 1)
        step(s)

    load_earlier.wait()
    for ch in range(CHUNKS):
        here = rows_of(0, 0, ch)
        total = own_sum(0, ch) + earlier[pl.ds(ch * PART, PART), :]
        arrived(down_recv.at[6, ch], down_rsem.at[6, ch])
        total += down_recv[6, ch]
        arrived(up_recv.at[7, ch], up_rsem.at[7, ch])
        total += up_recv[7, ch]
        out_ref[0, here, :] = total
        for j in (1, 3, 2):
            go(remote(out_ref.at[0, here, :], out_ref.at[0, here, :], o_ssem.at[j, ch], o_rsem.at[4 - j, ch], device(dy=j)))
        go(remote(out_ref.at[0, here, :], out_ref.at[0, here, :], o_ssem.at[4, ch], o_rsem.at[4, ch], device(dk=1)))
    for ch in range(CHUNKS):
        for j in (3, 1, 2):
            rows = rows_of(j, 0, ch)
            arrived(out_ref.at[0, rows, :], o_rsem.at[j, ch])
            go(remote(out_ref.at[0, rows, :], out_ref.at[0, rows, :], o_ssem.at[4 + j, ch], o_rsem.at[4 + j, ch], device(dk=1)))
    for ch in range(CHUNKS):
        for j in range(4):
            arrived(out_ref.at[0, rows_of(j, 1, ch), :], o_rsem.at[4 + j, ch])
    for copy in sends:
        copy.wait_send()


def body(half_tensor, earlier_blocks):
    vmem = pl.BlockSpec(memory_space=pltpu.VMEM)
    hbm = pl.BlockSpec(memory_space=pl.ANY)
    dma = pltpu.SemaphoreType.DMA
    return pl.pallas_call(
        kernel,
        out_shape=jax.ShapeDtypeStruct(earlier_blocks.shape, F32),
        in_specs=[hbm, hbm],
        out_specs=vmem,
        scratch_shapes=[
            pltpu.VMEM((ROWS * 32, 128), F32),
            pltpu.VMEM((OWN, WIDTH), F32),
            pltpu.VMEM((4, PIECE, 128), F32),
            pltpu.VMEM((4, PIECE, 128), F32),
            pltpu.VMEM((4, 8 * DEPTH, 128), F32),
            pltpu.VMEM((4, 8 * DEPTH, 128), F32),
            pltpu.VMEM((1024, DEPTH), BF16),
            pltpu.VMEM((1024, DEPTH), BF16),
            pltpu.VMEM((DEPTH, 1024), BF16),
            pltpu.VMEM((DEPTH, 1024), BF16),
            pltpu.VMEM((NZ, QUARTER, WIDTH), F32),
            pltpu.VMEM((NZ, OWN, WIDTH), F32),
            pltpu.VMEM((8, CHUNKS, PART, WIDTH), F32),
            pltpu.VMEM((7, CHUNKS, PART, WIDTH), F32),
            pltpu.VMEM((8, CHUNKS, PART, WIDTH), F32),
            pltpu.VMEM((7, CHUNKS, PART, WIDTH), F32),
            dma((2,)),
            dma((4, 5)),
            dma((4, 5)),
            dma((4, 5)),
            dma((5, 5)),
            dma((8,)),
            dma((8,)),
            dma((8, CHUNKS)),
            dma((8, CHUNKS)),
            dma((7, CHUNKS)),
            dma((7, CHUNKS)),
            dma((8, CHUNKS)),
            dma((8, CHUNKS)),
        ],
        compiler_params=pltpu.CompilerParams(
            collective_id=0, has_side_effects=True, vmem_limit_bytes=48 * 2**20
        ),
        cost_estimate=pl.CostEstimate(
            flops=6 * 1024 * 1024 * 16 * ROWS, bytes_accessed=3 * 2**20, transcendentals=0
        ),
    )(half_tensor.reshape(ROWS * 32, 128), earlier_blocks)


def solution(mesh):
    return jax.shard_map(
        body,
        mesh=mesh,
        in_specs=(P("row", "col", None), P("row", None, None)),
        out_specs=P("row", None, None),
        check_vma=False,
    )
```

```python
import jax
import jax.numpy as jnp
from jax import lax
from jax.experimental import pallas as pl
from jax.experimental.pallas import tpu as pltpu
from jax.sharding import PartitionSpec as P

MESH = pl.DeviceIdType.MESH
F32 = jnp.float32
BF16 = jnp.bfloat16

NX, NY, NZ, NK = 4, 4, 16, 2
ROWS = 50
PIECE = ROWS * 8
HALF = 25 * 8
DEPTH = 256
QUARTER = 128
OWN = 64
CHUNKS = 4
PART = OWN // CHUNKS
HALVED = (2,)
WIDTH = 512

GROUPS = (
    ((0, 0), (0, 3), (3, 0), (3, 3)),
    ((0, 1), (1, 0), (1, 1), (1, 3), (3, 1)),
    ((0, 2), (2, 0), (3, 2), (2, 3)),
    ((1, 2), (2, 1), (2, 2)),
)
PLACE = {source: (g, i) for g, group in enumerate(GROUPS) for i, source in enumerate(group)}
OFFSETS = (4, 3, 5, 2, 6, 1, 7, 0)


def kernel(
    half,
    earlier_hbm,
    out_ref,
    earlier,
    col_send,
    row_send,
    col_buf,
    row_buf,
    row_hi,
    row_lo,
    col_hi,
    col_lo,
    tile,
    sibling_tile,
    ring_send,
    ring_recv,
    in_sem,
    c_ssem,
    c_rsem,
    r_ssem,
    r_rsem,
    s_ssem,
    s_rsem,
    ring_ssem,
    ring_rsem,
    o_ssem,
    o_rsem,
):
    r = lax.axis_index("row")
    c = lax.axis_index("col")
    z, x, y, k = r // NX, r % NX, c // NK, c % NK
    odd = z % 2

    def device(dz=0, dx=0, dy=0, dk=0):
        return (
            lax.rem(z + dz, NZ) * NX + lax.rem(x + dx, NX),
            lax.rem(y + dy, NY) * NK + lax.rem(k + dk, NK),
        )

    def remote(src, dst, ssem, rsem, to):
        return pltpu.make_async_remote_copy(
            src_ref=src, dst_ref=dst, send_sem=ssem, recv_sem=rsem, device_id=to, device_id_type=MESH
        )

    def rows_of(dy, dk, chunk=None):
        start = lax.rem(y + dy, NY) * QUARTER + lax.rem(k + dk, NK) * OWN
        if chunk is None:
            return pl.ds(pl.multiple_of(start, OWN), OWN)
        return pl.ds(pl.multiple_of(start + chunk * PART, PART), PART)

    load_earlier = pltpu.make_async_copy(earlier_hbm.at[0, rows_of(0, 0), :], earlier, in_sem.at[0])
    load_earlier.start()

    peers = [device(dx=j) for j in range(1, NX)] + [device(dy=j) for j in range(1, NY)]
    peers += [device(dz=1), device(dz=NZ - 1), device(dk=1)]
    barrier = pltpu.get_barrier_semaphore()
    for peer in peers:
        pl.semaphore_signal(barrier, inc=1, device_id=peer, device_id_type=MESH)

    def slot(buf, dx, dy, part=None):
        group, i = PLACE[dx, dy]
        if part is None:
            return buf.at[group, pl.ds(i * PIECE, PIECE), :]
        return buf.at[group, pl.ds(i * PIECE + part * HALF, HALF), :]

    def prepare(j):
        n = lax.rem(x + j, NX)
        m = lax.rem(y + j, NY)
        for i in range(ROWS):
            col_send[j, pl.ds(8 * i, 4), :] = half[pl.ds(32 * i + 4 * n, 4), :]
            col_send[j, pl.ds(8 * i + 4, 4), :] = half[pl.ds(32 * i + 16 + 4 * n, 4), :]
            row_send[j, pl.ds(8 * i, 8), :] = half[pl.ds(32 * i + m, 8, stride=4), :]

    prepare(1)
    pl.semaphore_wait(barrier, len(peers))

    sends = []

    def go(copy):
        copy.start()
        sends.append(copy)

    for j in (1, 3, 2):
        if j != 1:
            prepare(j)
        go(remote(col_send.at[j], slot(col_buf, 4 - j, 0), c_ssem.at[j, 0], c_rsem.at[4 - j, 0], device(dx=j)))
        go(remote(row_send.at[j], slot(row_buf, 0, 4 - j), r_ssem.at[j, 0], r_rsem.at[0, 4 - j], device(dy=j)))
    prepare(0)
    slot(col_buf, 0, 0)[...] = col_send[0]
    slot(row_buf, 0, 0)[...] = row_send[0]

    def spread(a):
        for part, up, down in ((0, 1, 2), (1, 5, 6)) if a in HALVED else ((None, 1, 2),):
            other = None if part is None else 1 - part
            up_to = 3 if up == 1 else 5
            down_to = 1 if down == 2 else 6
            go(remote(slot(col_buf, a, 0, part), slot(col_buf, a, 3, part), c_ssem.at[a, up], c_rsem.at[a, up_to], device(dy=1)))
            go(remote(slot(row_buf, 0, a, part), slot(row_buf, 3, a, part), r_ssem.at[a, up], r_rsem.at[up_to, a], device(dx=1)))
            go(remote(slot(col_buf, a, 0, other), slot(col_buf, a, 1, other), c_ssem.at[a, down], c_rsem.at[a, down_to], device(dy=3)))
            go(remote(slot(row_buf, 0, a, other), slot(row_buf, 1, a, other), r_ssem.at[a, down], r_rsem.at[down_to, a], device(dx=3)))

    def arrived(dst, rsem):
        remote(dst, dst, rsem, rsem, device(dy=1)).wait_recv()

    def forward(a):
        low, high = (0, 1) if a in HALVED else (None, None)
        arrived(slot(col_buf, a, 3, low), c_rsem.at[a, 3])
        go(remote(slot(col_buf, a, 3, 0), slot(col_buf, a, 2, 0), c_ssem.at[a, 3], c_rsem.at[a, 2], device(dy=1)))
        arrived(slot(row_buf, 3, a, low), r_rsem.at[3, a])
        go(remote(slot(row_buf, 3, a, 0), slot(row_buf, 2, a, 0), r_ssem.at[a, 3], r_rsem.at[2, a], device(dx=1)))
        arrived(slot(col_buf, a, 1, high), c_rsem.at[a, 1])
        go(remote(slot(col_buf, a, 1, 1), slot(col_buf, a, 2, 1), c_ssem.at[a, 4], c_rsem.at[a, 4], device(dy=3)))
        arrived(slot(row_buf, 1, a, high), r_rsem.at[1, a])
        go(remote(slot(row_buf, 1, a, 1), slot(row_buf, 2, a, 1), r_ssem.at[a, 4], r_rsem.at[4, a], device(dx=3)))
        if a in HALVED:
            arrived(slot(col_buf, a, 3, 1), c_rsem.at[a, 5])
            arrived(slot(row_buf, 3, a, 1), r_rsem.at[5, a])
            arrived(slot(col_buf, a, 1, 0), c_rsem.at[a, 6])
            arrived(slot(row_buf, 1, a, 0), r_rsem.at[6, a])

    def finish(a):
        arrived(slot(col_buf, a, 2, 0), c_rsem.at[a, 2])
        arrived(slot(row_buf, 2, a, 0), r_rsem.at[2, a])
        arrived(slot(col_buf, a, 2, 1), c_rsem.at[a, 4])
        arrived(slot(row_buf, 2, a, 1), r_rsem.at[4, a])

    def split(g):
        for n in range(8):
            v = col_buf[g, pl.ds(n, DEPTH, stride=8), :]
            hi = v.astype(BF16)
            col_hi[:, 128 * n : 128 * n + 128] = hi
            col_lo[:, 128 * n : 128 * n + 128] = (v - hi.astype(F32)).astype(BF16)
            offset = odd * ((8 - OFFSETS[n]) % 8) + (1 - odd) * OFFSETS[n]
            u = lax.rem(z // 2 + offset, 8)
            v = row_buf[g, pl.ds(u, DEPTH, stride=8), :].T
            hi = v.astype(BF16)
            row_hi[128 * n : 128 * n + 128, :] = hi
            row_lo[128 * n : 128 * n + 128, :] = (v - hi.astype(F32)).astype(BF16)

    def product(rows, cols):
        acc = jnp.dot(row_lo[rows, :], col_hi[:, cols], preferred_element_type=F32)
        acc += jnp.dot(row_hi[rows, :], col_lo[:, cols], preferred_element_type=F32)
        acc += jnp.dot(row_hi[rows, :], col_hi[:, cols], preferred_element_type=F32)
        return acc

    def multiply(g):
        split(g)

        @pl.loop(0, 4)
        def _(j):
            acc = product(slice(None), pl.ds(pl.multiple_of(j * 256, 256), 256))
            cols = pl.ds(pl.multiple_of((j % 2) * 256, 256), 256)
            for n in range(8):
                part = acc[128 * n : 128 * n + 128]
                if g > 0:
                    part += tile[2 * n + j // 2, :, cols]
                tile[2 * n + j // 2, :, cols] = part

    spread(0)
    for g, group in enumerate(GROUPS):
        filled = len(group) * PIECE
        pad = jnp.zeros((8 * DEPTH - filled, 128), F32)
        col_buf[g, pl.ds(filled, 8 * DEPTH - filled), :] = pad
        row_buf[g, pl.ds(filled, 8 * DEPTH - filled), :] = pad
    for a in (3, 1, 2):
        arrived(slot(col_buf, a, 0), c_rsem.at[a, 0])
        arrived(slot(row_buf, 0, a), r_rsem.at[0, a])
        spread(a)
        if a == 3:
            forward(0)
    forward(3)
    multiply(0)
    forward(1)
    multiply(1)
    forward(2)
    finish(0)
    finish(3)
    multiply(2)
    finish(1)
    finish(2)
    split(3)

    other = pl.ds(pl.multiple_of((1 - k) * OWN, OWN), OWN)

    def last(m):
        for j in range(4):
            acc = product(slice(256 * m, 256 * m + 256), slice(256 * j, 256 * j + 256))
            cols = slice((j % 2) * 256, (j % 2) * 256 + 256)
            for n in range(2):
                tile[4 * m + 2 * n + j // 2, :, cols] += acc[128 * n : 128 * n + 128]
        for n in (2 * m, 2 * m + 1):
            go(remote(tile.at[pl.ds(2 * n, 2), other, :], sibling_tile.at[pl.ds(2 * n, 2)], s_ssem.at[n], s_rsem.at[n], device(dk=1)))

    def sibling_arrived(n):
        arrived(sibling_tile.at[pl.ds(2 * n, 2)], s_rsem.at[n])

    def own_sum(way, distance, chunk):
        def slot_of(dz):
            n = 2 * OFFSETS.index(dz // 2) + dz % 2
            return (1 - odd) * n + odd * (n + 1 - 2 * (n % 2))

        side = (way + k + odd) % 2
        n = (1 - side) * slot_of(distance) + side * slot_of((NZ - distance) % NZ)
        mine = pl.ds(pl.multiple_of(k * OWN + chunk * PART, PART), PART)
        return tile[n, mine, :] + sibling_tile[n, pl.ds(chunk * PART, PART), :]

    def step(s):
        for i in range(2, CHUNKS) if s == 0 else range(CHUNKS):
            for way in range(2):
                ch = (i + 2 * (1 - way)) % CHUNKS
                total = own_sum(way, 8 - s, ch)
                if s > 1 or (s == 1 and i > 1):
                    arrived(ring_recv.at[way, s - 1, ch], ring_rsem.at[way, s - 1, ch])
                    total += ring_recv[way, s - 1, ch]
                ring_send[way, s, ch] = total
                to = device(dz=1 + 14 * ((way + k) % 2))
                go(remote(ring_send.at[way, s, ch], ring_recv.at[way, s, ch], ring_ssem.at[way, s, ch], ring_rsem.at[way, s, ch], to))

    last(0)
    last(1)
    sibling_arrived(0)
    sibling_arrived(1)
    step(0)
    last(2)
    sibling_arrived(2)
    step(1)
    last(3)
    sibling_arrived(3)
    step(2)
    for s in range(3, 8):
        if s < 7:
            sibling_arrived(s + 1)
        step(s)

    load_earlier.wait()
    for ch in range(CHUNKS):
        total = own_sum(0, 0, ch) + earlier[pl.ds(ch * PART, PART), :]
        for way in range(2):
            arrived(ring_recv.at[way, 7, ch], ring_rsem.at[way, 7, ch])
            total += ring_recv[way, 7, ch]
        here = rows_of(0, 0, ch)
        out_ref[0, here, :] = total
        for j in (2, 1, 3):
            go(remote(out_ref.at[0, here, :], out_ref.at[0, here, :], o_ssem.at[j, ch], o_rsem.at[4 - j, ch], device(dy=j)))
        go(remote(out_ref.at[0, here, :], out_ref.at[0, here, :], o_ssem.at[4, ch], o_rsem.at[4, ch], device(dk=1)))
    for ch in range(CHUNKS):
        for j in (3, 1, 2):
            rows = rows_of(j, 0, ch)
            arrived(out_ref.at[0, rows, :], o_rsem.at[j, ch])
            go(remote(out_ref.at[0, rows, :], out_ref.at[0, rows, :], o_ssem.at[4 + j, ch], o_rsem.at[4 + j, ch], device(dk=1)))
    for ch in range(CHUNKS):
        for j in range(4):
            arrived(out_ref.at[0, rows_of(j, 1, ch), :], o_rsem.at[4 + j, ch])
    for copy in sends:
        copy.wait_send()


def body(half_tensor, earlier_blocks):
    vmem = pl.BlockSpec(memory_space=pltpu.VMEM)
    hbm = pl.BlockSpec(memory_space=pl.ANY)
    dma = pltpu.SemaphoreType.DMA
    return pl.pallas_call(
        kernel,
        out_shape=jax.ShapeDtypeStruct(earlier_blocks.shape, F32),
        in_specs=[vmem, hbm],
        out_specs=vmem,
        scratch_shapes=[
            pltpu.VMEM((OWN, WIDTH), F32),
            pltpu.VMEM((4, PIECE, 128), F32),
            pltpu.VMEM((4, PIECE, 128), F32),
            pltpu.VMEM((4, 8 * DEPTH, 128), F32),
            pltpu.VMEM((4, 8 * DEPTH, 128), F32),
            pltpu.VMEM((1024, DEPTH), BF16),
            pltpu.VMEM((1024, DEPTH), BF16),
            pltpu.VMEM((DEPTH, 1024), BF16),
            pltpu.VMEM((DEPTH, 1024), BF16),
            pltpu.VMEM((NZ, QUARTER, WIDTH), F32),
            pltpu.VMEM((NZ, OWN, WIDTH), F32),
            pltpu.VMEM((2, 8, CHUNKS, PART, WIDTH), F32),
            pltpu.VMEM((2, 8, CHUNKS, PART, WIDTH), F32),
            dma((1,)),
            dma((4, 7)),
            dma((4, 7)),
            dma((4, 7)),
            dma((7, 5)),
            dma((8,)),
            dma((8,)),
            dma((2, 8, CHUNKS)),
            dma((2, 8, CHUNKS)),
            dma((8, CHUNKS)),
            dma((8, CHUNKS)),
        ],
        compiler_params=pltpu.CompilerParams(
            collective_id=0, has_side_effects=True, vmem_limit_bytes=52 * 2**20
        ),
        cost_estimate=pl.CostEstimate(
            flops=6 * 1024 * 1024 * 16 * ROWS, bytes_accessed=3 * 2**20, transcendentals=0
        ),
    )(half_tensor.reshape(ROWS * 32, 128), earlier_blocks)


def solution(mesh):
    return jax.shard_map(
        body,
        mesh=mesh,
        in_specs=(P("row", "col", None), P("row", None, None)),
        out_specs=P("row", None, None),
        check_vma=False,
    )
```

```python
import jax
import jax.numpy as jnp
from jax import lax
from jax.experimental import pallas as pl
from jax.experimental.pallas import tpu as pltpu
from jax.sharding import PartitionSpec as P

MESH = pl.DeviceIdType.MESH
F32 = jnp.float32
BF16 = jnp.bfloat16

NX, NY, NZ, NK = 4, 4, 16, 2
ROWS = 50
PIECE = ROWS * 8
HALF = 25 * 8
DEPTH = 256
QUARTER = 128
OWN = 64
CHUNKS = 4
PART = OWN // CHUNKS
WIDTH = 512

GROUPS = (
    ((0, 0), (0, 3), (3, 0), (3, 3)),
    ((0, 1), (1, 0), (1, 1), (1, 3), (3, 1)),
    ((0, 2), (2, 0), (3, 2), (2, 3)),
    ((1, 2), (2, 1), (2, 2)),
)
PLACE = {source: (g, i) for g, group in enumerate(GROUPS) for i, source in enumerate(group)}
OFFSETS = (4, 3, 5, 2, 6, 1, 7, 0)


def kernel(
    half,
    earlier_hbm,
    out_ref,
    earlier,
    col_send,
    row_send,
    col_buf,
    row_buf,
    row_hi,
    row_lo,
    col_hi,
    col_lo,
    tile,
    sibling_tile,
    ring_send,
    ring_recv,
    in_sem,
    c_ssem,
    c_rsem,
    r_ssem,
    r_rsem,
    s_ssem,
    s_rsem,
    ring_ssem,
    ring_rsem,
    o_ssem,
    o_rsem,
):
    r = lax.axis_index("row")
    c = lax.axis_index("col")
    z, x, y, k = r // NX, r % NX, c // NK, c % NK
    odd = z % 2

    def device(dz=0, dx=0, dy=0, dk=0):
        return (
            lax.rem(z + dz, NZ) * NX + lax.rem(x + dx, NX),
            lax.rem(y + dy, NY) * NK + lax.rem(k + dk, NK),
        )

    def remote(src, dst, ssem, rsem, to):
        return pltpu.make_async_remote_copy(
            src_ref=src, dst_ref=dst, send_sem=ssem, recv_sem=rsem, device_id=to, device_id_type=MESH
        )

    def rows_of(dy, dk, chunk=None):
        start = lax.rem(y + dy, NY) * QUARTER + lax.rem(k + dk, NK) * OWN
        if chunk is None:
            return pl.ds(pl.multiple_of(start, OWN), OWN)
        return pl.ds(pl.multiple_of(start + chunk * PART, PART), PART)

    load_earlier = pltpu.make_async_copy(earlier_hbm.at[0, rows_of(0, 0), :], earlier, in_sem.at[0])
    load_earlier.start()

    peers = [device(dx=j) for j in range(1, NX)] + [device(dy=j) for j in range(1, NY)]
    peers += [device(dz=1), device(dz=NZ - 1), device(dk=1)]
    barrier = pltpu.get_barrier_semaphore()
    for peer in peers:
        pl.semaphore_signal(barrier, inc=1, device_id=peer, device_id_type=MESH)

    def slot(buf, dx, dy, part=None):
        group, i = PLACE[dx, dy]
        if part is None:
            return buf.at[group, pl.ds(i * PIECE, PIECE), :]
        return buf.at[group, pl.ds(i * PIECE + part * HALF, HALF), :]

    def prepare(j):
        n = lax.rem(x + j, NX)
        m = lax.rem(y + j, NY)
        for i in range(ROWS):
            col_send[j, pl.ds(8 * i, 4), :] = half[pl.ds(32 * i + 4 * n, 4), :]
            col_send[j, pl.ds(8 * i + 4, 4), :] = half[pl.ds(32 * i + 16 + 4 * n, 4), :]
            row_send[j, pl.ds(8 * i, 8), :] = half[pl.ds(32 * i + m, 8, stride=4), :]

    for j in (1, 3, 2, 0):
        prepare(j)
    pl.semaphore_wait(barrier, len(peers))

    sends = []

    def go(copy):
        copy.start()
        sends.append(copy)

    def drain(left, most):
        for _ in range(min(most, len(sends) - left)):
            sends.pop(0).wait_send()

    for j in (1, 3, 2):
        go(remote(col_send.at[j], slot(col_buf, 4 - j, 0), c_ssem.at[j, 0], c_rsem.at[4 - j, 0], device(dx=j)))
        go(remote(row_send.at[j], slot(row_buf, 0, 4 - j), r_ssem.at[j, 0], r_rsem.at[0, 4 - j], device(dy=j)))
    slot(col_buf, 0, 0)[...] = col_send[0]
    slot(row_buf, 0, 0)[...] = row_send[0]

    def spread(a):
        go(remote(slot(col_buf, a, 0), slot(col_buf, a, 3), c_ssem.at[a, 1], c_rsem.at[a, 3], device(dy=1)))
        go(remote(slot(row_buf, 0, a), slot(row_buf, 3, a), r_ssem.at[a, 1], r_rsem.at[3, a], device(dx=1)))
        go(remote(slot(col_buf, a, 0), slot(col_buf, a, 1), c_ssem.at[a, 2], c_rsem.at[a, 1], device(dy=3)))
        go(remote(slot(row_buf, 0, a), slot(row_buf, 1, a), r_ssem.at[a, 2], r_rsem.at[1, a], device(dx=3)))

    def arrived(dst, rsem):
        remote(dst, dst, rsem, rsem, device(dy=1)).wait_recv()

    def forward(a):
        arrived(slot(col_buf, a, 3), c_rsem.at[a, 3])
        go(remote(slot(col_buf, a, 3, 0), slot(col_buf, a, 2, 0), c_ssem.at[a, 3], c_rsem.at[a, 2], device(dy=1)))
        arrived(slot(row_buf, 3, a), r_rsem.at[3, a])
        go(remote(slot(row_buf, 3, a, 0), slot(row_buf, 2, a, 0), r_ssem.at[a, 3], r_rsem.at[2, a], device(dx=1)))
        arrived(slot(col_buf, a, 1), c_rsem.at[a, 1])
        go(remote(slot(col_buf, a, 1, 1), slot(col_buf, a, 2, 1), c_ssem.at[a, 4], c_rsem.at[a, 4], device(dy=3)))
        arrived(slot(row_buf, 1, a), r_rsem.at[1, a])
        go(remote(slot(row_buf, 1, a, 1), slot(row_buf, 2, a, 1), r_ssem.at[a, 4], r_rsem.at[4, a], device(dx=3)))

    def finish(a):
        arrived(slot(col_buf, a, 2, 0), c_rsem.at[a, 2])
        arrived(slot(row_buf, 2, a, 0), r_rsem.at[2, a])
        arrived(slot(col_buf, a, 2, 1), c_rsem.at[a, 4])
        arrived(slot(row_buf, 2, a, 1), r_rsem.at[4, a])

    def split(g):
        for n in range(8):
            v = col_buf[g, pl.ds(n, DEPTH, stride=8), :]
            hi = v.astype(BF16)
            col_hi[:, 128 * n : 128 * n + 128] = hi
            col_lo[:, 128 * n : 128 * n + 128] = (v - hi.astype(F32)).astype(BF16)
            offset = odd * ((8 - OFFSETS[n]) % 8) + (1 - odd) * OFFSETS[n]
            u = lax.rem(z // 2 + offset, 8)
            v = row_buf[g, pl.ds(u, DEPTH, stride=8), :].T
            hi = v.astype(BF16)
            row_hi[128 * n : 128 * n + 128, :] = hi
            row_lo[128 * n : 128 * n + 128, :] = (v - hi.astype(F32)).astype(BF16)

    def product(rows, cols):
        acc = jnp.dot(row_lo[rows, :], col_hi[:, cols], preferred_element_type=F32)
        acc += jnp.dot(row_hi[rows, :], col_lo[:, cols], preferred_element_type=F32)
        acc += jnp.dot(row_hi[rows, :], col_hi[:, cols], preferred_element_type=F32)
        return acc

    def multiply(g):
        split(g)

        @pl.loop(0, 4)
        def _(j):
            acc = product(slice(None), pl.ds(pl.multiple_of(j * 256, 256), 256))
            cols = pl.ds(pl.multiple_of((j % 2) * 256, 256), 256)
            for n in range(8):
                part = acc[128 * n : 128 * n + 128]
                if g > 0:
                    part += tile[2 * n + j // 2, :, cols]
                tile[2 * n + j // 2, :, cols] = part

    spread(0)
    for g, group in enumerate(GROUPS):
        filled = len(group) * PIECE
        pad = jnp.zeros((8 * DEPTH - filled, 128), F32)
        col_buf[g, pl.ds(filled, 8 * DEPTH - filled), :] = pad
        row_buf[g, pl.ds(filled, 8 * DEPTH - filled), :] = pad
    for a in (3, 1, 2):
        arrived(slot(col_buf, a, 0), c_rsem.at[a, 0])
        arrived(slot(row_buf, 0, a), r_rsem.at[0, a])
        spread(a)
        if a == 3:
            forward(0)
    forward(3)
    multiply(0)
    forward(1)
    multiply(1)
    forward(2)
    finish(0)
    finish(3)
    multiply(2)
    finish(1)
    finish(2)
    split(3)

    other = pl.ds(pl.multiple_of((1 - k) * OWN, OWN), OWN)

    def last(m):
        for j in range(2):
            acc = product(slice(512 * m, 512 * m + 512), slice(512 * j, 512 * j + 512))
            for n in range(4):
                tile[8 * m + 2 * n + j] += acc[128 * n : 128 * n + 128]
        for n in range(4 * m, 4 * m + 4):
            go(remote(tile.at[pl.ds(2 * n, 2), other, :], sibling_tile.at[pl.ds(2 * n, 2)], s_ssem.at[n], s_rsem.at[n], device(dk=1)))

    def sibling_arrived(n):
        arrived(sibling_tile.at[pl.ds(2 * n, 2)], s_rsem.at[n])

    def own_sum(way, distance, chunk):
        def slot_of(dz):
            n = 2 * OFFSETS.index(dz // 2) + dz % 2
            return (1 - odd) * n + odd * (n + 1 - 2 * (n % 2))

        side = (way + k + odd) % 2
        n = (1 - side) * slot_of(distance) + side * slot_of((NZ - distance) % NZ)
        mine = pl.ds(pl.multiple_of(k * OWN + chunk * PART, PART), PART)
        return tile[n, mine, :] + sibling_tile[n, pl.ds(chunk * PART, PART), :]

    def step(s):
        for i in range(2, CHUNKS) if s == 0 else range(CHUNKS):
            for way in range(2):
                ch = (i + 2 * (1 - way)) % CHUNKS
                total = own_sum(way, 8 - s, ch)
                if s > 1 or (s == 1 and i > 1):
                    arrived(ring_recv.at[way, s - 1, ch], ring_rsem.at[way, s - 1, ch])
                    total += ring_recv[way, s - 1, ch]
                ring_send[way, s, ch] = total
                to = device(dz=1 + 14 * ((way + k) % 2))
                go(remote(ring_send.at[way, s, ch], ring_recv.at[way, s, ch], ring_ssem.at[way, s, ch], ring_rsem.at[way, s, ch], to))

    last(0)
    sibling_arrived(0)
    sibling_arrived(1)
    step(0)
    last(1)
    sibling_arrived(2)
    step(1)
    sibling_arrived(3)
    step(2)
    drain(16, 24)
    for s in range(3, 8):
        if s < 7:
            sibling_arrived(s + 1)
        step(s)
        drain(8, 24)

    load_earlier.wait()
    for ch in range(CHUNKS):
        total = own_sum(0, 0, ch) + earlier[pl.ds(ch * PART, PART), :]
        for way in range(2):
            arrived(ring_recv.at[way, 7, ch], ring_rsem.at[way, 7, ch])
            total += ring_recv[way, 7, ch]
        here = rows_of(0, 0, ch)
        out_ref[0, here, :] = total
        for j in (2, 1, 3):
            go(remote(out_ref.at[0, here, :], out_ref.at[0, here, :], o_ssem.at[j, ch], o_rsem.at[4 - j, ch], device(dy=j)))
        go(remote(out_ref.at[0, here, :], out_ref.at[0, here, :], o_ssem.at[4, ch], o_rsem.at[4, ch], device(dk=1)))
    for ch in range(CHUNKS):
        for j in (3, 1, 2):
            rows = rows_of(j, 0, ch)
            arrived(out_ref.at[0, rows, :], o_rsem.at[j, ch])
            go(remote(out_ref.at[0, rows, :], out_ref.at[0, rows, :], o_ssem.at[4 + j, ch], o_rsem.at[4 + j, ch], device(dk=1)))
    for ch in range(CHUNKS):
        for j in range(4):
            arrived(out_ref.at[0, rows_of(j, 1, ch), :], o_rsem.at[4 + j, ch])
    for copy in sends:
        copy.wait_send()


def body(half_tensor, earlier_blocks):
    vmem = pl.BlockSpec(memory_space=pltpu.VMEM)
    hbm = pl.BlockSpec(memory_space=pl.ANY)
    dma = pltpu.SemaphoreType.DMA
    return pl.pallas_call(
        kernel,
        out_shape=jax.ShapeDtypeStruct(earlier_blocks.shape, F32),
        in_specs=[vmem, hbm],
        out_specs=vmem,
        scratch_shapes=[
            pltpu.VMEM((OWN, WIDTH), F32),
            pltpu.VMEM((4, PIECE, 128), F32),
            pltpu.VMEM((4, PIECE, 128), F32),
            pltpu.VMEM((4, 8 * DEPTH, 128), F32),
            pltpu.VMEM((4, 8 * DEPTH, 128), F32),
            pltpu.VMEM((1024, DEPTH), BF16),
            pltpu.VMEM((1024, DEPTH), BF16),
            pltpu.VMEM((DEPTH, 1024), BF16),
            pltpu.VMEM((DEPTH, 1024), BF16),
            pltpu.VMEM((NZ, QUARTER, WIDTH), F32),
            pltpu.VMEM((NZ, OWN, WIDTH), F32),
            pltpu.VMEM((2, 8, CHUNKS, PART, WIDTH), F32),
            pltpu.VMEM((2, 8, CHUNKS, PART, WIDTH), F32),
            dma((1,)),
            dma((4, 5)),
            dma((4, 5)),
            dma((4, 5)),
            dma((5, 5)),
            dma((8,)),
            dma((8,)),
            dma((2, 8, CHUNKS)),
            dma((2, 8, CHUNKS)),
            dma((8, CHUNKS)),
            dma((8, CHUNKS)),
        ],
        compiler_params=pltpu.CompilerParams(
            collective_id=0, has_side_effects=True, vmem_limit_bytes=52 * 2**20
        ),
        cost_estimate=pl.CostEstimate(
            flops=6 * 1024 * 1024 * 16 * ROWS, bytes_accessed=3 * 2**20, transcendentals=0
        ),
    )(half_tensor.reshape(ROWS * 32, 128), earlier_blocks)


def solution(mesh):
    return jax.shard_map(
        body,
        mesh=mesh,
        in_specs=(P("row", "col", None), P("row", None, None)),
        out_specs=P("row", None, None),
        check_vma=False,
    )
```

```python
import jax
import jax.numpy as jnp
from jax import lax
from jax.experimental import pallas as pl
from jax.experimental.pallas import tpu as pltpu
from jax.sharding import PartitionSpec as P

MESH = pl.DeviceIdType.MESH
F32 = jnp.float32
BF16 = jnp.bfloat16

NX, NY, NZ, NK = 4, 4, 16, 2
ROWS = 50
PIECE = ROWS * 8
HALF = 25 * 8
DEPTH = 256
LAST = 128
QUARTER = 128
OWN = 64
CHUNKS = 4
PART = OWN // CHUNKS
WIDTH = 512

GROUPS = (
    ((0, 0), (0, 3), (3, 0), (3, 3)),
    ((0, 1), (1, 0), (1, 1), (1, 3), (3, 1)),
    ((0, 2), (2, 0), (3, 2), (2, 3), (1, 2)),
    ((2, 1), (2, 2)),
)
PLACE = {source: (g, i) for g, group in enumerate(GROUPS) for i, source in enumerate(group)}
OFFSETS = (4, 3, 5, 2, 6, 1, 7, 0)


def kernel(
    half,
    earlier_hbm,
    out_ref,
    earlier,
    col_send,
    row_send,
    col_buf,
    row_buf,
    row_hi,
    row_lo,
    col_hi,
    col_lo,
    tile,
    sibling_tile,
    ring_send,
    ring_recv,
    in_sem,
    c_ssem,
    c_rsem,
    r_ssem,
    r_rsem,
    s_ssem,
    s_rsem,
    ring_ssem,
    ring_rsem,
    o_ssem,
    o_rsem,
):
    r = lax.axis_index("row")
    c = lax.axis_index("col")
    z, x, y, k = r // NX, r % NX, c // NK, c % NK
    odd = z % 2

    def device(dz=0, dx=0, dy=0, dk=0):
        return (
            lax.rem(z + dz, NZ) * NX + lax.rem(x + dx, NX),
            lax.rem(y + dy, NY) * NK + lax.rem(k + dk, NK),
        )

    def remote(src, dst, ssem, rsem, to):
        return pltpu.make_async_remote_copy(
            src_ref=src, dst_ref=dst, send_sem=ssem, recv_sem=rsem, device_id=to, device_id_type=MESH
        )

    def rows_of(dy, dk, chunk=None):
        start = lax.rem(y + dy, NY) * QUARTER + lax.rem(k + dk, NK) * OWN
        if chunk is None:
            return pl.ds(pl.multiple_of(start, OWN), OWN)
        return pl.ds(pl.multiple_of(start + chunk * PART, PART), PART)

    load_earlier = pltpu.make_async_copy(earlier_hbm.at[0, rows_of(0, 0), :], earlier, in_sem.at[0])
    load_earlier.start()

    peers = [device(dx=j) for j in range(1, NX)] + [device(dy=j) for j in range(1, NY)]
    peers += [device(dz=1), device(dz=NZ - 1), device(dk=1)]
    barrier = pltpu.get_barrier_semaphore()
    for peer in peers:
        pl.semaphore_signal(barrier, inc=1, device_id=peer, device_id_type=MESH)

    def slot(buf, dx, dy, part=None):
        group, i = PLACE[dx, dy]
        if part is None:
            return buf.at[group, pl.ds(i * PIECE, PIECE), :]
        return buf.at[group, pl.ds(i * PIECE + part * HALF, HALF), :]

    def prepare(j):
        n = lax.rem(x + j, NX)
        m = lax.rem(y + j, NY)
        for i in range(ROWS):
            col_send[j, pl.ds(8 * i, 4), :] = half[pl.ds(32 * i + 4 * n, 4), :]
            col_send[j, pl.ds(8 * i + 4, 4), :] = half[pl.ds(32 * i + 16 + 4 * n, 4), :]
            row_send[j, pl.ds(8 * i, 8), :] = half[pl.ds(32 * i + m, 8, stride=4), :]

    for j in (1, 3, 2, 0):
        prepare(j)
    pl.semaphore_wait(barrier, len(peers))

    sends = []

    def go(copy):
        copy.start()
        sends.append(copy)

    def drain(left, most):
        for _ in range(min(most, len(sends) - left)):
            sends.pop(0).wait_send()

    for j in (1, 3, 2):
        go(remote(col_send.at[j], slot(col_buf, 4 - j, 0), c_ssem.at[j, 0], c_rsem.at[4 - j, 0], device(dx=j)))
        go(remote(row_send.at[j], slot(row_buf, 0, 4 - j), r_ssem.at[j, 0], r_rsem.at[0, 4 - j], device(dy=j)))
    slot(col_buf, 0, 0)[...] = col_send[0]
    slot(row_buf, 0, 0)[...] = row_send[0]

    def spread(a):
        go(remote(slot(col_buf, a, 0), slot(col_buf, a, 3), c_ssem.at[a, 1], c_rsem.at[a, 3], device(dy=1)))
        go(remote(slot(row_buf, 0, a), slot(row_buf, 3, a), r_ssem.at[a, 1], r_rsem.at[3, a], device(dx=1)))
        go(remote(slot(col_buf, a, 0), slot(col_buf, a, 1), c_ssem.at[a, 2], c_rsem.at[a, 1], device(dy=3)))
        go(remote(slot(row_buf, 0, a), slot(row_buf, 1, a), r_ssem.at[a, 2], r_rsem.at[1, a], device(dx=3)))

    def arrived(dst, rsem):
        remote(dst, dst, rsem, rsem, device(dy=1)).wait_recv()

    def forward(a):
        arrived(slot(col_buf, a, 3), c_rsem.at[a, 3])
        go(remote(slot(col_buf, a, 3, 0), slot(col_buf, a, 2, 0), c_ssem.at[a, 3], c_rsem.at[a, 2], device(dy=1)))
        arrived(slot(row_buf, 3, a), r_rsem.at[3, a])
        go(remote(slot(row_buf, 3, a, 0), slot(row_buf, 2, a, 0), r_ssem.at[a, 3], r_rsem.at[2, a], device(dx=1)))
        arrived(slot(col_buf, a, 1), c_rsem.at[a, 1])
        go(remote(slot(col_buf, a, 1, 1), slot(col_buf, a, 2, 1), c_ssem.at[a, 4], c_rsem.at[a, 4], device(dy=3)))
        arrived(slot(row_buf, 1, a), r_rsem.at[1, a])
        go(remote(slot(row_buf, 1, a, 1), slot(row_buf, 2, a, 1), r_ssem.at[a, 4], r_rsem.at[4, a], device(dx=3)))

    def finish(a):
        arrived(slot(col_buf, a, 2, 0), c_rsem.at[a, 2])
        arrived(slot(row_buf, 2, a, 0), r_rsem.at[2, a])
        arrived(slot(col_buf, a, 2, 1), c_rsem.at[a, 4])
        arrived(slot(row_buf, 2, a, 1), r_rsem.at[4, a])

    def split(g, depth=DEPTH):
        for n in range(8):
            v = col_buf[g, pl.ds(n, depth, stride=8), :]
            hi = v.astype(BF16)
            col_hi[:depth, 128 * n : 128 * n + 128] = hi
            col_lo[:depth, 128 * n : 128 * n + 128] = (v - hi.astype(F32)).astype(BF16)
            offset = odd * ((8 - OFFSETS[n]) % 8) + (1 - odd) * OFFSETS[n]
            u = lax.rem(z // 2 + offset, 8)
            v = row_buf[g, pl.ds(u, depth, stride=8), :].T
            hi = v.astype(BF16)
            row_hi[128 * n : 128 * n + 128, :depth] = hi
            row_lo[128 * n : 128 * n + 128, :depth] = (v - hi.astype(F32)).astype(BF16)

    def product(rows, cols, depth=DEPTH):
        acc = jnp.dot(row_lo[rows, :depth], col_hi[:depth, cols], preferred_element_type=F32)
        acc += jnp.dot(row_hi[rows, :depth], col_lo[:depth, cols], preferred_element_type=F32)
        acc += jnp.dot(row_hi[rows, :depth], col_hi[:depth, cols], preferred_element_type=F32)
        return acc

    def multiply(g):
        split(g)

        @pl.loop(0, 4)
        def _(j):
            acc = product(slice(None), pl.ds(pl.multiple_of(j * 256, 256), 256))
            cols = pl.ds(pl.multiple_of((j % 2) * 256, 256), 256)
            for n in range(8):
                part = acc[128 * n : 128 * n + 128]
                if g > 0:
                    part += tile[2 * n + j // 2, :, cols]
                tile[2 * n + j // 2, :, cols] = part

    spread(0)
    for g, group in enumerate(GROUPS):
        filled = len(group) * PIECE
        pad = jnp.zeros((8 * DEPTH - filled, 128), F32)
        col_buf[g, pl.ds(filled, 8 * DEPTH - filled), :] = pad
        row_buf[g, pl.ds(filled, 8 * DEPTH - filled), :] = pad
    for a in (3, 1, 2):
        arrived(slot(col_buf, a, 0), c_rsem.at[a, 0])
        arrived(slot(row_buf, 0, a), r_rsem.at[0, a])
        spread(a)
        if a == 3:
            forward(0)
    forward(3)
    multiply(0)
    forward(1)
    multiply(1)
    forward(2)
    finish(0)
    finish(3)
    finish(1)
    multiply(2)
    finish(2)
    split(3, LAST)

    other = pl.ds(pl.multiple_of((1 - k) * OWN, OWN), OWN)

    def last(m):
        for j in range(2):
            acc = product(slice(512 * m, 512 * m + 512), slice(512 * j, 512 * j + 512), LAST)
            for n in range(4):
                tile[8 * m + 2 * n + j] += acc[128 * n : 128 * n + 128]
        for n in range(4 * m, 4 * m + 4):
            go(remote(tile.at[pl.ds(2 * n, 2), other, :], sibling_tile.at[pl.ds(2 * n, 2)], s_ssem.at[n], s_rsem.at[n], device(dk=1)))

    def sibling_arrived(n):
        arrived(sibling_tile.at[pl.ds(2 * n, 2)], s_rsem.at[n])

    def own_sum(way, distance, chunk):
        def slot_of(dz):
            n = 2 * OFFSETS.index(dz // 2) + dz % 2
            return (1 - odd) * n + odd * (n + 1 - 2 * (n % 2))

        side = (way + k + odd) % 2
        n = (1 - side) * slot_of(distance) + side * slot_of((NZ - distance) % NZ)
        mine = pl.ds(pl.multiple_of(k * OWN + chunk * PART, PART), PART)
        return tile[n, mine, :] + sibling_tile[n, pl.ds(chunk * PART, PART), :]

    def step(s):
        for i in range(2, CHUNKS) if s == 0 else range(CHUNKS):
            for way in range(2):
                ch = (i + 2 * (1 - way)) % CHUNKS
                total = own_sum(way, 8 - s, ch)
                if s > 1 or (s == 1 and i > 1):
                    arrived(ring_recv.at[way, s - 1, ch], ring_rsem.at[way, s - 1, ch])
                    total += ring_recv[way, s - 1, ch]
                ring_send[way, s, ch] = total
                to = device(dz=1 + 14 * ((way + k) % 2))
                go(remote(ring_send.at[way, s, ch], ring_recv.at[way, s, ch], ring_ssem.at[way, s, ch], ring_rsem.at[way, s, ch], to))

    last(0)
    sibling_arrived(0)
    sibling_arrived(1)
    step(0)
    last(1)
    sibling_arrived(2)
    step(1)
    sibling_arrived(3)
    step(2)
    drain(16, 24)
    for s in range(3, 8):
        if s < 7:
            sibling_arrived(s + 1)
        step(s)
        drain(8, 24)

    load_earlier.wait()
    for ch in range(CHUNKS):
        total = own_sum(0, 0, ch) + earlier[pl.ds(ch * PART, PART), :]
        for way in range(2):
            arrived(ring_recv.at[way, 7, ch], ring_rsem.at[way, 7, ch])
            total += ring_recv[way, 7, ch]
        here = rows_of(0, 0, ch)
        out_ref[0, here, :] = total
        for j in (2, 1, 3):
            go(remote(out_ref.at[0, here, :], out_ref.at[0, here, :], o_ssem.at[j, ch], o_rsem.at[4 - j, ch], device(dy=j)))
        go(remote(out_ref.at[0, here, :], out_ref.at[0, here, :], o_ssem.at[4, ch], o_rsem.at[4, ch], device(dk=1)))
    for ch in range(CHUNKS):
        for j in (3, 1, 2):
            rows = rows_of(j, 0, ch)
            arrived(out_ref.at[0, rows, :], o_rsem.at[j, ch])
            go(remote(out_ref.at[0, rows, :], out_ref.at[0, rows, :], o_ssem.at[4 + j, ch], o_rsem.at[4 + j, ch], device(dk=1)))
    for ch in range(CHUNKS):
        for j in range(4):
            arrived(out_ref.at[0, rows_of(j, 1, ch), :], o_rsem.at[4 + j, ch])
    for copy in sends:
        copy.wait_send()


def body(half_tensor, earlier_blocks):
    vmem = pl.BlockSpec(memory_space=pltpu.VMEM)
    hbm = pl.BlockSpec(memory_space=pl.ANY)
    dma = pltpu.SemaphoreType.DMA
    return pl.pallas_call(
        kernel,
        out_shape=jax.ShapeDtypeStruct(earlier_blocks.shape, F32),
        in_specs=[vmem, hbm],
        out_specs=vmem,
        scratch_shapes=[
            pltpu.VMEM((OWN, WIDTH), F32),
            pltpu.VMEM((4, PIECE, 128), F32),
            pltpu.VMEM((4, PIECE, 128), F32),
            pltpu.VMEM((4, 8 * DEPTH, 128), F32),
            pltpu.VMEM((4, 8 * DEPTH, 128), F32),
            pltpu.VMEM((1024, DEPTH), BF16),
            pltpu.VMEM((1024, DEPTH), BF16),
            pltpu.VMEM((DEPTH, 1024), BF16),
            pltpu.VMEM((DEPTH, 1024), BF16),
            pltpu.VMEM((NZ, QUARTER, WIDTH), F32),
            pltpu.VMEM((NZ, OWN, WIDTH), F32),
            pltpu.VMEM((2, 8, CHUNKS, PART, WIDTH), F32),
            pltpu.VMEM((2, 8, CHUNKS, PART, WIDTH), F32),
            dma((1,)),
            dma((4, 5)),
            dma((4, 5)),
            dma((4, 5)),
            dma((5, 5)),
            dma((8,)),
            dma((8,)),
            dma((2, 8, CHUNKS)),
            dma((2, 8, CHUNKS)),
            dma((8, CHUNKS)),
            dma((8, CHUNKS)),
        ],
        compiler_params=pltpu.CompilerParams(
            collective_id=0, has_side_effects=True, vmem_limit_bytes=52 * 2**20
        ),
        cost_estimate=pl.CostEstimate(
            flops=6 * 1024 * 1024 * 16 * ROWS, bytes_accessed=3 * 2**20, transcendentals=0
        ),
    )(half_tensor.reshape(ROWS * 32, 128), earlier_blocks)


def solution(mesh):
    return jax.shard_map(
        body,
        mesh=mesh,
        in_specs=(P("row", "col", None), P("row", None, None)),
        out_specs=P("row", None, None),
        check_vma=False,
    )
```

```python
import jax
import jax.numpy as jnp
from jax import lax
from jax.experimental import pallas as pl
from jax.experimental.pallas import tpu as pltpu
from jax.sharding import PartitionSpec as P

MESH = pl.DeviceIdType.MESH
F32 = jnp.float32
BF16 = jnp.bfloat16

NX, NY, NZ, NK = 4, 4, 16, 2
ROWS = 50
PIECE = ROWS * 8
HALF = 25 * 8
DEPTH = 256
QUARTER = 128
OWN = 64
CHUNKS = 4
PART = OWN // CHUNKS
WIDTH = 512

GROUPS = (
    ((0, 0), (0, 3), (3, 0), (3, 3)),
    ((0, 1), (1, 0), (1, 1), (1, 3), (3, 1)),
    ((0, 2), (2, 0), (3, 2), (2, 3)),
    ((1, 2), (2, 1), (2, 2)),
)
PLACE = {source: (g, i) for g, group in enumerate(GROUPS) for i, source in enumerate(group)}
OFFSETS = (4, 3, 5, 2, 6, 1, 7, 0)


def kernel(
    half,
    earlier_hbm,
    out_ref,
    earlier,
    col_send,
    row_send,
    col_buf,
    row_buf,
    row_hi,
    row_lo,
    col_hi,
    col_lo,
    tile,
    sibling_tile,
    ring_send,
    ring_recv,
    in_sem,
    c_ssem,
    c_rsem,
    r_ssem,
    r_rsem,
    s_ssem,
    s_rsem,
    ring_ssem,
    ring_rsem,
    o_ssem,
    o_rsem,
):
    r = lax.axis_index("row")
    c = lax.axis_index("col")
    z, x, y, k = r // NX, r % NX, c // NK, c % NK
    odd = z % 2

    def device(dz=0, dx=0, dy=0, dk=0):
        return (
            lax.rem(z + dz, NZ) * NX + lax.rem(x + dx, NX),
            lax.rem(y + dy, NY) * NK + lax.rem(k + dk, NK),
        )

    def remote(src, dst, ssem, rsem, to):
        return pltpu.make_async_remote_copy(
            src_ref=src, dst_ref=dst, send_sem=ssem, recv_sem=rsem, device_id=to, device_id_type=MESH
        )

    def rows_of(dy, dk, chunk=None):
        start = lax.rem(y + dy, NY) * QUARTER + lax.rem(k + dk, NK) * OWN
        if chunk is None:
            return pl.ds(pl.multiple_of(start, OWN), OWN)
        return pl.ds(pl.multiple_of(start + chunk * 2 * PART, 2 * PART), 2 * PART)

    load_earlier = pltpu.make_async_copy(earlier_hbm.at[0, rows_of(0, 0), :], earlier, in_sem.at[0])
    load_earlier.start()

    peers = [device(dx=j) for j in range(1, NX)] + [device(dy=j) for j in range(1, NY)]
    peers += [device(dz=1), device(dz=NZ - 1), device(dk=1)]
    barrier = pltpu.get_barrier_semaphore()
    for peer in peers:
        pl.semaphore_signal(barrier, inc=1, device_id=peer, device_id_type=MESH)

    def slot(buf, dx, dy, part=None):
        group, i = PLACE[dx, dy]
        if part is None:
            return buf.at[group, pl.ds(i * PIECE, PIECE), :]
        return buf.at[group, pl.ds(i * PIECE + part * HALF, HALF), :]

    def prepare(j):
        n = lax.rem(x + j, NX)
        m = lax.rem(y + j, NY)
        for i in range(ROWS):
            col_send[j, pl.ds(8 * i, 4), :] = half[pl.ds(32 * i + 4 * n, 4), :]
            col_send[j, pl.ds(8 * i + 4, 4), :] = half[pl.ds(32 * i + 16 + 4 * n, 4), :]
            row_send[j, pl.ds(8 * i, 8), :] = half[pl.ds(32 * i + m, 8, stride=4), :]

    for j in (1, 3, 2, 0):
        prepare(j)
    pl.semaphore_wait(barrier, len(peers))

    sends = []

    def go(copy):
        copy.start()
        sends.append(copy)

    def drain(left, most):
        for _ in range(min(most, len(sends) - left)):
            sends.pop(0).wait_send()

    for j in (1, 3, 2):
        go(remote(col_send.at[j], slot(col_buf, 4 - j, 0), c_ssem.at[j, 0], c_rsem.at[4 - j, 0], device(dx=j)))
        go(remote(row_send.at[j], slot(row_buf, 0, 4 - j), r_ssem.at[j, 0], r_rsem.at[0, 4 - j], device(dy=j)))
    slot(col_buf, 0, 0)[...] = col_send[0]
    slot(row_buf, 0, 0)[...] = row_send[0]

    def spread(a):
        go(remote(slot(col_buf, a, 0), slot(col_buf, a, 3), c_ssem.at[a, 1], c_rsem.at[a, 3], device(dy=1)))
        go(remote(slot(row_buf, 0, a), slot(row_buf, 3, a), r_ssem.at[a, 1], r_rsem.at[3, a], device(dx=1)))
        go(remote(slot(col_buf, a, 0), slot(col_buf, a, 1), c_ssem.at[a, 2], c_rsem.at[a, 1], device(dy=3)))
        go(remote(slot(row_buf, 0, a), slot(row_buf, 1, a), r_ssem.at[a, 2], r_rsem.at[1, a], device(dx=3)))

    def arrived(dst, rsem):
        remote(dst, dst, rsem, rsem, device(dy=1)).wait_recv()

    def forward(a):
        arrived(slot(col_buf, a, 3), c_rsem.at[a, 3])
        go(remote(slot(col_buf, a, 3, 0), slot(col_buf, a, 2, 0), c_ssem.at[a, 3], c_rsem.at[a, 2], device(dy=1)))
        arrived(slot(row_buf, 3, a), r_rsem.at[3, a])
        go(remote(slot(row_buf, 3, a, 0), slot(row_buf, 2, a, 0), r_ssem.at[a, 3], r_rsem.at[2, a], device(dx=1)))
        arrived(slot(col_buf, a, 1), c_rsem.at[a, 1])
        go(remote(slot(col_buf, a, 1, 1), slot(col_buf, a, 2, 1), c_ssem.at[a, 4], c_rsem.at[a, 4], device(dy=3)))
        arrived(slot(row_buf, 1, a), r_rsem.at[1, a])
        go(remote(slot(row_buf, 1, a, 1), slot(row_buf, 2, a, 1), r_ssem.at[a, 4], r_rsem.at[4, a], device(dx=3)))

    def finish(a):
        arrived(slot(col_buf, a, 2, 0), c_rsem.at[a, 2])
        arrived(slot(row_buf, 2, a, 0), r_rsem.at[2, a])
        arrived(slot(col_buf, a, 2, 1), c_rsem.at[a, 4])
        arrived(slot(row_buf, 2, a, 1), r_rsem.at[4, a])

    def split(g):
        for n in range(8):
            v = col_buf[g, pl.ds(n, DEPTH, stride=8), :]
            hi = v.astype(BF16)
            col_hi[:, 128 * n : 128 * n + 128] = hi
            col_lo[:, 128 * n : 128 * n + 128] = (v - hi.astype(F32)).astype(BF16)
            offset = odd * ((8 - OFFSETS[n]) % 8) + (1 - odd) * OFFSETS[n]
            u = lax.rem(z // 2 + offset, 8)
            v = row_buf[g, pl.ds(u, DEPTH, stride=8), :].T
            hi = v.astype(BF16)
            row_hi[128 * n : 128 * n + 128, :] = hi
            row_lo[128 * n : 128 * n + 128, :] = (v - hi.astype(F32)).astype(BF16)

    def product(rows, cols):
        acc = jnp.dot(row_lo[rows, :], col_hi[:, cols], preferred_element_type=F32)
        acc += jnp.dot(row_hi[rows, :], col_lo[:, cols], preferred_element_type=F32)
        acc += jnp.dot(row_hi[rows, :], col_hi[:, cols], preferred_element_type=F32)
        return acc

    def multiply(g):
        split(g)

        @pl.loop(0, 4)
        def _(j):
            acc = product(slice(None), pl.ds(pl.multiple_of(j * 256, 256), 256))
            cols = pl.ds(pl.multiple_of((j % 2) * 256, 256), 256)
            for n in range(8):
                part = acc[128 * n : 128 * n + 128]
                if g > 0:
                    part += tile[2 * n + j // 2, :, cols]
                tile[2 * n + j // 2, :, cols] = part

    spread(0)
    for g, group in enumerate(GROUPS):
        filled = len(group) * PIECE
        pad = jnp.zeros((8 * DEPTH - filled, 128), F32)
        col_buf[g, pl.ds(filled, 8 * DEPTH - filled), :] = pad
        row_buf[g, pl.ds(filled, 8 * DEPTH - filled), :] = pad
    for a in (3, 1, 2):
        arrived(slot(col_buf, a, 0), c_rsem.at[a, 0])
        arrived(slot(row_buf, 0, a), r_rsem.at[0, a])
        spread(a)
        if a == 3:
            forward(0)
    forward(3)
    multiply(0)
    forward(1)
    multiply(1)
    forward(2)
    finish(0)
    finish(3)
    multiply(2)
    finish(1)
    finish(2)
    split(3)

    other = pl.ds(pl.multiple_of((1 - k) * OWN, OWN), OWN)

    def last(m):
        for j in range(2):
            acc = product(slice(512 * m, 512 * m + 512), slice(512 * j, 512 * j + 512))
            for n in range(4):
                tile[8 * m + 2 * n + j] += acc[128 * n : 128 * n + 128]
        for n in range(4 * m, 4 * m + 4):
            go(remote(tile.at[pl.ds(2 * n, 2), other, :], sibling_tile.at[pl.ds(2 * n, 2)], s_ssem.at[n], s_rsem.at[n], device(dk=1)))

    def sibling_arrived(n):
        arrived(sibling_tile.at[pl.ds(2 * n, 2)], s_rsem.at[n])

    def own_sum(way, distance, chunk):
        def slot_of(dz):
            n = 2 * OFFSETS.index(dz // 2) + dz % 2
            return (1 - odd) * n + odd * (n + 1 - 2 * (n % 2))

        side = (way + k + odd) % 2
        n = (1 - side) * slot_of(distance) + side * slot_of((NZ - distance) % NZ)
        mine = pl.ds(pl.multiple_of(k * OWN + chunk * PART, PART), PART)
        return tile[n, mine, :] + sibling_tile[n, pl.ds(chunk * PART, PART), :]

    def step(s):
        for i in range(2, CHUNKS) if s == 0 else range(CHUNKS):
            for way in range(2):
                ch = (i + 2 * (1 - way)) % CHUNKS
                total = own_sum(way, 8 - s, ch)
                if s > 1 or (s == 1 and i > 1):
                    arrived(ring_recv.at[way, s - 1, ch], ring_rsem.at[way, s - 1, ch])
                    total += ring_recv[way, s - 1, ch]
                ring_send[way, s, ch] = total
                to = device(dz=1 + 14 * ((way + k) % 2))
                go(remote(ring_send.at[way, s, ch], ring_recv.at[way, s, ch], ring_ssem.at[way, s, ch], ring_rsem.at[way, s, ch], to))

    last(0)
    sibling_arrived(0)
    sibling_arrived(1)
    step(0)
    last(1)
    sibling_arrived(2)
    step(1)
    sibling_arrived(3)
    step(2)
    drain(16, 24)
    for s in range(3, 8):
        if s < 7:
            sibling_arrived(s + 1)
        step(s)
        drain(8, 24)

    load_earlier.wait()
    for ch in range(CHUNKS):
        total = own_sum(0, 0, ch) + earlier[pl.ds(ch * PART, PART), :]
        for way in range(2):
            arrived(ring_recv.at[way, 7, ch], ring_rsem.at[way, 7, ch])
            total += ring_recv[way, 7, ch]
        start = y * QUARTER + k * OWN + ch * PART
        out_ref[0, pl.ds(pl.multiple_of(start, PART), PART), :] = total
        if ch % 2 == 1:
            part = ch // 2
            block = out_ref.at[0, rows_of(0, 0, part), :]
            for j in (2, 1, 3):
                go(remote(block, block, o_ssem.at[j, part], o_rsem.at[4 - j, part], device(dy=j)))
            go(remote(block, block, o_ssem.at[4, part], o_rsem.at[4, part], device(dk=1)))
    for part in range(CHUNKS // 2):
        for j in (3, 1, 2):
            block = out_ref.at[0, rows_of(j, 0, part), :]
            arrived(block, o_rsem.at[j, part])
            go(remote(block, block, o_ssem.at[4 + j, part], o_rsem.at[4 + j, part], device(dk=1)))
    for part in range(CHUNKS // 2):
        for j in range(4):
            arrived(out_ref.at[0, rows_of(j, 1, part), :], o_rsem.at[4 + j, part])
    for copy in sends:
        copy.wait_send()


def body(half_tensor, earlier_blocks):
    vmem = pl.BlockSpec(memory_space=pltpu.VMEM)
    hbm = pl.BlockSpec(memory_space=pl.ANY)
    dma = pltpu.SemaphoreType.DMA
    return pl.pallas_call(
        kernel,
        out_shape=jax.ShapeDtypeStruct(earlier_blocks.shape, F32),
        in_specs=[vmem, hbm],
        out_specs=vmem,
        scratch_shapes=[
            pltpu.VMEM((OWN, WIDTH), F32),
            pltpu.VMEM((4, PIECE, 128), F32),
            pltpu.VMEM((4, PIECE, 128), F32),
            pltpu.VMEM((4, 8 * DEPTH, 128), F32),
            pltpu.VMEM((4, 8 * DEPTH, 128), F32),
            pltpu.VMEM((1024, DEPTH), BF16),
            pltpu.VMEM((1024, DEPTH), BF16),
            pltpu.VMEM((DEPTH, 1024), BF16),
            pltpu.VMEM((DEPTH, 1024), BF16),
            pltpu.VMEM((NZ, QUARTER, WIDTH), F32),
            pltpu.VMEM((NZ, OWN, WIDTH), F32),
            pltpu.VMEM((2, 8, CHUNKS, PART, WIDTH), F32),
            pltpu.VMEM((2, 8, CHUNKS, PART, WIDTH), F32),
            dma((1,)),
            dma((4, 5)),
            dma((4, 5)),
            dma((4, 5)),
            dma((5, 5)),
            dma((8,)),
            dma((8,)),
            dma((2, 8, CHUNKS)),
            dma((2, 8, CHUNKS)),
            dma((8, CHUNKS // 2)),
            dma((8, CHUNKS // 2)),
        ],
        compiler_params=pltpu.CompilerParams(
            collective_id=0, has_side_effects=True, vmem_limit_bytes=52 * 2**20
        ),
        cost_estimate=pl.CostEstimate(
            flops=6 * 1024 * 1024 * 16 * ROWS, bytes_accessed=3 * 2**20, transcendentals=0
        ),
    )(half_tensor.reshape(ROWS * 32, 128), earlier_blocks)


def solution(mesh):
    return jax.shard_map(
        body,
        mesh=mesh,
        in_specs=(P("row", "col", None), P("row", None, None)),
        out_specs=P("row", None, None),
        check_vma=False,
    )
```
